512 devices in a mesh: dp: 4 (over x), row: 16 (over y, core), col: 8 (over z).
Axes of the slice: x: 4, y: 8, z: 8, core: 2. Of those that a mesh axis runs over, the one named last changes fastest.
Arguments:
- grad_wi: bfloat16 [4, 4096, 16384], P('dp', 'row', 'col'), may hold values from -100 to 100
- grad_wo: bfloat16 [4, 16384, 4096], P('dp', 'row', 'col'), may hold values from -100 to 100
- row_wi: float32 [4096], P('row'), may hold values from 0.01 to 1
- col_wi: float32 [16384], P('col'), may hold values from 0.01 to 1
- row_wo: float32 [16384], P('row'), may hold values from 0.01 to 1
- col_wo: float32 [4096], P('col'), may hold values from 0.01 to 1
Outputs:
- update_wi: bfloat16 [4096, 16384], P('row', 'col')
- row_wi_new: float32 [4096], P('row')
- col_wi_new: float32 [16384], P('col')
- update_wo: bfloat16 [16384, 4096], P('row', 'col')
- row_wo_new: float32 [16384], P('row')
- col_wo_new: float32 [4096], P('col')
The draws below stay inside these ranges and needn't reach their ends.
All inputs are finite; a program needn't handle non-finite values.
Results may differ from the reference program's by a relative error of at most 0.015.
Values may be sent and summed in bfloat16 or wider, within the bound.
A program may use at most 64 MiB of HBM per device.

```python
import math
import jax
import jax.numpy as jnp
from jax import lax

D = 4096
FF = 16384
N_DP = 4


LOG_HOT = 2.77


def tile_levels(key, count):
    tile_draws = jax.random.uniform(key, (count // 64,), jnp.float32, 0.0, 1.0)
    hot_level = jnp.clip(3.0 * tile_draws - 1.0, 0.0, 1.0)
    return jnp.repeat(hot_level, 64)


def make_gradient(key, groups, rows, cols):
    keys = jax.random.split(key, 7)
    ramp_rows = jnp.sqrt(1.0 + 2.0 * jnp.arange(rows, dtype=jnp.float32) / rows)
    ramp_cols = jnp.sqrt(1.0 + 2.0 * jnp.arange(cols, dtype=jnp.float32) / cols)
    row_scale = jnp.exp(jax.random.uniform(keys[0], (rows,), jnp.float32, -0.9, 0.9)) * ramp_rows
    col_scale = jnp.exp(jax.random.uniform(keys[1], (cols,), jnp.float32, -0.9, 0.9)) * ramp_cols
    row_level = tile_levels(keys[5], rows)
    col_level = tile_levels(keys[6], cols)
    joint_factor = jnp.exp(0.5 * LOG_HOT * row_level[:, None] * col_level[None, :])
    noise = jnp.clip(jax.random.normal(keys[2], (groups, rows, cols), jnp.float32), -5.0, 5.0)
    values = 0.2 * noise * row_scale[None, :, None] * col_scale[None, None, :] * joint_factor[None, :, :]
    values = jnp.clip(values, -100.0, 100.0)
    return values.astype(jnp.bfloat16)


def draw_grad_wi(key, part):
    return make_gradient(jax.random.fold_in(key, 11), N_DP, D, FF)


def draw_grad_wo(key, part):
    return make_gradient(jax.random.fold_in(key, 23), N_DP, FF, D)


def steps_of(own_key, dims, pieces, least, largest):
    gain = 1.0
    for axis_at, shards_of in pieces:
        draws = jax.random.uniform(jax.random.fold_in(jax.random.fold_in(own_key, 6), axis_at), (shards_of,), jnp.float32, least / len(pieces), largest / len(pieces))
        gain = gain * jnp.repeat(jnp.exp(draws), dims[axis_at] // shards_of).reshape((-1,) + (1,) * (len(dims) - 1 - axis_at))
    return gain


def setup_inputs(seed: int = 0) -> dict:
    seeds = jax.random.split(jax.random.key(seed), 7)
    return {
        "grad_wi": draw_grad_wi(jax.random.fold_in(seeds[6], 71), 0),
        "grad_wo": draw_grad_wo(jax.random.fold_in(seeds[6], 71), 0),
        "row_wi": jnp.clip(jnp.exp(math.log(1.0) - 4.6051702 * jax.random.uniform(seeds[2], (D,), jnp.float32) ** steps_of(seeds[2], (D,), ((0, 16),), -0.2, 0.2)), 0.01, 1.0),
        "col_wi": jnp.clip(jnp.exp(math.log(1.0) - 4.6051702 * jax.random.uniform(seeds[3], (FF,), jnp.float32) ** steps_of(seeds[3], (FF,), ((0, 8),), -0.2, 0.2)), 0.01, 1.0),
        "row_wo": jnp.clip(jnp.exp(math.log(1.0) - 4.6051702 * jax.random.uniform(seeds[4], (FF,), jnp.float32) ** steps_of(seeds[4], (FF,), ((0, 16),), -0.2, 0.2)), 0.01, 1.0),
        "col_wo": jnp.clip(jnp.exp(math.log(1.0) - 4.6051702 * jax.random.uniform(seeds[5], (D,), jnp.float32) ** steps_of(seeds[5], (D,), ((0, 8),), -0.2, 0.2)), 0.01, 1.0),
    }


BETA = 0.8
EPS_SQUARE = 1e-30

def factored(grad, row_prev, col_prev):
    total = lax.optimization_barrier(jnp.sum(grad.astype(jnp.float32), axis=0))
    squares = total * total + EPS_SQUARE
    row_new = BETA * row_prev + (1.0 - BETA) * lax.optimization_barrier(jnp.mean(squares, axis=1))
    col_new = BETA * col_prev + (1.0 - BETA) * lax.optimization_barrier(jnp.mean(squares, axis=0))
    second = row_new[:, None] * col_new[None, :]
    raw = total / jnp.sqrt(second)
    rms_value = jnp.sqrt(jnp.mean(raw * raw))
    update = (raw / jnp.maximum(1.0, rms_value)).astype(jnp.bfloat16)
    return (update, row_new, col_new)

def reference(grad_wi, grad_wo, row_wi, col_wi, row_wo, col_wo):
    update_wi, row_wi_new, col_wi_new = factored(grad_wi, row_wi, col_wi)
    update_wo, row_wo_new, col_wo_new = factored(grad_wo, row_wo, col_wo)
    return (update_wi, row_wi_new, col_wi_new, update_wo, row_wo_new, col_wo_new)
```

```python
import functools

import jax
import jax.numpy as jnp
from jax import lax
from jax.experimental import pallas as pl
from jax.experimental.pallas import tpu as pltpu
from jax.sharding import PartitionSpec as P

BETA = 0.8
EPS_SQUARE = 1e-30
N_DP = 4
HALF = 128
PIECE = 2 * HALF
WIDE = 512
LANES = 128
TILES = WIDE // LANES
ROWS = 64
CHUNKS = HALF // ROWS

MESH = pl.DeviceIdType.MESH
FORWARD, BACKWARD = 0, 1


def kernel(
    n_row,
    n_col,
    grad_wi,
    grad_wo,
    row_wi,
    col_wi,
    row_wo,
    col_wo,
    update_wi,
    row_wi_new,
    col_wi_new,
    update_wo,
    row_wo_new,
    col_wo_new,
    own,
    near,
    passing,
    direct,
    combined,
    total,
    squares,
    row_part,
    col_part,
    z_sums,
    y_sums,
    x_sums,
    row_scale,
    col_scale_wi,
    col_scale_wo,
    z_energy,
    y_energy,
    x_energy,
    load_sem,
    big_send,
    passing_recv,
    direct_recv,
    combined_recv,
    gather_recv,
    onward_recv,
    small_send,
    small_recv,
):
    me = lax.axis_index("dp")
    my_row = lax.axis_index("row")
    my_col = lax.axis_index("col")
    right = lax.rem(me + 1, N_DP)
    left = lax.rem(me + N_DP - 1, N_DP)
    across = lax.rem(me + 2, N_DP)
    target = (right, left)

    def rows_at(c):
        return pl.ds(pl.multiple_of(c * ROWS, ROWS), ROWS)

    def grad_at(m, piece, start, size):
        if m == 0:
            return grad_wi.at[
                0, pl.ds(start, size), pl.ds(pl.multiple_of(piece * WIDE, WIDE), WIDE)
            ]
        return grad_wo.at[
            0, pl.ds(pl.multiple_of(piece * PIECE + start, ROWS), size), :
        ]

    def grad_chunk(m, piece, half, c):
        return grad_at(m, piece, pl.multiple_of(half * HALF + c * ROWS, ROWS), ROWS)

    loads = []
    for m in range(2):
        loads.append(pltpu.make_async_copy(grad_at(m, right, 0, HALF), near.at[FORWARD, m], load_sem.at[m]))
        loads.append(pltpu.make_async_copy(grad_at(m, left, HALF, HALF), near.at[BACKWARD, m], load_sem.at[2 + m]))
        loads.append(pltpu.make_async_copy(grad_at(m, me, 0, PIECE), own.at[m], load_sem.at[4 + m]))
    for load in loads:
        load.start()

    barrier = pltpu.get_barrier_semaphore()

    def greet(axis, n, index):
        def body(d, carry):
            pl.semaphore_signal(
                barrier, inc=1, device_id={axis: lax.rem(index + d, n)}, device_id_type=MESH
            )
            return carry

        lax.fori_loop(1, n, body, 0)

    greet("dp", N_DP, me)
    greet("row", n_row, my_row)
    greet("col", n_col, my_col)
    pl.semaphore_wait(barrier, N_DP + n_row + n_col - 3)

    def send(src, dst, send_sem, recv_sem, to):
        return pltpu.make_async_remote_copy(
            src_ref=src,
            dst_ref=dst,
            send_sem=send_sem,
            recv_sem=recv_sem,
            device_id={"dp": to},
            device_id_type=MESH,
        )

    for m in range(2):

        @pl.loop(0, CHUNKS)
        def _(c):
            for way in (FORWARD, BACKWARD):
                send(
                    grad_chunk(m, across, way, c),
                    passing.at[way, m, rows_at(c)],
                    big_send.at[0],
                    passing_recv.at[way, m, c],
                    target[way],
                ).start()

    for m in range(2):

        @pl.loop(0, CHUNKS)
        def _(c):
            for way in (FORWARD, BACKWARD):
                send(
                    grad_chunk(m, target[way], 1 - way, c),
                    direct.at[way, m, rows_at(c)],
                    big_send.at[1],
                    direct_recv.at[way, m, c],
                    target[way],
                ).start()

    for load in loads:
        load.wait()

    for m in range(2):

        @pl.loop(0, CHUNKS)
        def _(c):
            for way in (FORWARD, BACKWARD):
                here = passing.at[way, m, rows_at(c)]
                send(here, here, big_send.at[0], passing_recv.at[way, m, c], target[way]).wait_recv()
                here[...] = (
                    here[...].astype(jnp.float32) + near[way, m, rows_at(c)].astype(jnp.float32)
                ).astype(jnp.bfloat16)
                send(
                    here,
                    combined.at[way, m, rows_at(c)],
                    big_send.at[2],
                    combined_recv.at[way, m, c],
                    target[way],
                ).start()

    def gather(m, half, c, way):
        part = total.at[me, m, pl.ds(pl.multiple_of(half * HALF + c * ROWS, ROWS), ROWS)]
        return send(part, part, big_send.at[3 + half], gather_recv.at[way, m, half, c], target[way])

    for m in range(2):
        col_part[m] = jnp.zeros((8, WIDE), jnp.float32)

        @pl.loop(0, CHUNKS)
        def _(c):
            for way in (FORWARD, BACKWARD):
                half = way
                first = direct.at[1 - way, m, rows_at(c)]
                second = combined.at[way, m, rows_at(c)]
                send(first, first, big_send.at[1], direct_recv.at[1 - way, m, c], right).wait_recv()
                send(second, second, big_send.at[2], combined_recv.at[way, m, c], right).wait_recv()
                rows = pl.ds(pl.multiple_of(half * HALF + c * ROWS, ROWS), ROWS)
                value = (
                    own[m, rows].astype(jnp.float32)
                    + first[...].astype(jnp.float32)
                    + second[...].astype(jnp.float32)
                )
                total[me, m, rows] = value.astype(jnp.bfloat16)
                gather(m, half, c, way).start()
                square = value * value
                squares[m, rows] = square
                row_part[m, rows] = sum(
                    square[:, k * LANES : (k + 1) * LANES] for k in range(TILES)
                )
                col_part[m] += jnp.sum(square.reshape(ROWS // 8, 8, WIDE), axis=0)

    for m in range(2):

        @pl.loop(0, CHUNKS)
        def _(c):
            for way in (FORWARD, BACKWARD):
                gather(m, 1 - way, c, way).start()

    def exchange_start(buffer, n, axis, index, at):
        def body(d, carry):
            pltpu.make_async_remote_copy(
                src_ref=buffer.at[index],
                dst_ref=buffer.at[index],
                send_sem=small_send.at[at],
                recv_sem=small_recv.at[at],
                device_id={axis: lax.rem(index + d, n)},
                device_id_type=MESH,
            ).start()
            return carry

        lax.fori_loop(1, n, body, 0)

    def exchange_wait(buffer, n, axis, index, at):
        others = buffer.at[pl.ds(0, n - 1)]
        pltpu.make_async_copy(others, others, small_recv.at[at]).wait()
        pltpu.make_async_copy(others, others, small_send.at[at]).wait()

    for m in range(2):
        for half in range(2):
            block = row_part[m, half * HALF : (half + 1) * HALF].T
            z_sums[my_col, m * 2 + half : m * 2 + half + 1] = jnp.sum(block, axis=0, keepdims=True)
    exchange_start(z_sums, n_col, "col", my_col, 0)
    for m in range(2):
        column = jnp.sum(col_part[m], axis=0, keepdims=True)
        for k in range(TILES):
            y_sums[my_row, m * TILES + k : m * TILES + k + 1] = column[:, k * LANES : (k + 1) * LANES]
    exchange_start(y_sums, n_row, "row", my_row, 1)
    exchange_wait(z_sums, n_col, "col", my_col, 0)
    exchange_wait(y_sums, n_row, "row", my_row, 1)

    def add_up(buffer, n):
        result = buffer[0]
        for j in range(1, n):
            result = result + buffer[j]
        return result

    x_sums[me, 0:4] = add_up(z_sums, n_col)
    x_sums[me, 8:16] = add_up(y_sums, n_row)
    exchange_start(x_sums, N_DP, "dp", me, 2)
    exchange_wait(x_sums, N_DP, "dp", me, 2)

    def mix(previous, sums, count):
        return BETA * previous + (1.0 - BETA) * (sums * (1.0 / count) + EPS_SQUARE)

    by_x = [x_sums[x] for x in range(N_DP)]
    rows_wi, rows_wo = n_row * PIECE, n_row * PIECE * N_DP
    cols_wi, cols_wo = n_col * WIDE * N_DP, n_col * WIDE
    new = mix(row_wi[...], by_x[0][0:2] + by_x[1][0:2] + by_x[2][0:2] + by_x[3][0:2], cols_wi)
    row_wi_new[...] = new
    factor_wi = lax.rsqrt(new)
    new = mix(row_wo[...], jnp.concatenate([x[2:4] for x in by_x], axis=0), cols_wo)
    row_wo_new[...] = new
    factor_wo = lax.rsqrt(new)
    for half in range(2):
        row_scale[half] = jnp.broadcast_to(factor_wi[half : half + 1], (LANES, LANES)).T
    for half in range(2 * N_DP):
        row_scale[2 + half] = jnp.broadcast_to(factor_wo[half : half + 1], (LANES, LANES)).T
    new = mix(col_wi[...], jnp.concatenate([x[8:12] for x in by_x], axis=0), rows_wi)
    col_wi_new[...] = new
    col_scale_wi[...] = lax.rsqrt(new)
    new = mix(col_wo[...], by_x[0][12:16] + by_x[1][12:16] + by_x[2][12:16] + by_x[3][12:16], rows_wo)
    col_wo_new[...] = new
    col_scale_wo[...] = lax.rsqrt(new)

    for m in range(2):

        @pl.loop(0, CHUNKS)
        def _(c):
            for way in (FORWARD, BACKWARD):
                source = target[1 - way]
                half = way
                part = total.at[source, m, pl.ds(pl.multiple_of(half * HALF + c * ROWS, ROWS), ROWS)]
                send(part, part, big_send.at[3], gather_recv.at[way, m, half, c], right).wait_recv()
                send(part, part, big_send.at[5], onward_recv.at[way, m, c], target[way]).start()

    for m in range(2):
        energy = jnp.zeros((HALF, LANES), jnp.float32)
        for half in range(2):
            weighted = jnp.zeros((HALF, LANES), jnp.float32)
            for k in range(TILES):
                if m == 0:
                    column = col_scale_wi[pl.ds(me * TILES + k, 1)]
                else:
                    column = col_scale_wo[k : k + 1]
                weighted += squares[m, half * HALF : (half + 1) * HALF, k * LANES : (k + 1) * LANES] * (
                    column * column
                )
            scale = row_scale[half] if m == 0 else row_scale[2 + me * 2 + half]
            energy += weighted * (scale * scale)
        z_energy[my_col, m : m + 1] = jnp.sum(energy, axis=0, keepdims=True)
    exchange_start(z_energy, n_col, "col", my_col, 3)
    exchange_wait(z_energy, n_col, "col", my_col, 3)
    y_energy[my_row] = add_up(z_energy, n_col)
    exchange_start(y_energy, n_row, "row", my_row, 4)
    exchange_wait(y_energy, n_row, "row", my_row, 4)
    x_energy[me] = add_up(y_energy, n_row)
    exchange_start(x_energy, N_DP, "dp", me, 5)
    exchange_wait(x_energy, N_DP, "dp", me, 5)
    energy = jnp.sum(add_up(x_energy, N_DP), axis=1, keepdims=True)
    clip = 1.0 / jnp.maximum(1.0, jnp.sqrt(energy * (1.0 / (rows_wi * cols_wi))))
    col_scale_wi[...] = col_scale_wi[...] * clip[0:1]
    col_scale_wo[...] = col_scale_wo[...] * clip[1:2]

    def finish(piece, m, half, c):
        rows = pl.ds(pl.multiple_of(half * HALF + c * ROWS, ROWS), ROWS)
        value = total[piece, m, rows].astype(jnp.float32)
        if m == 0:
            scale = row_scale[half, rows_at(c)]
        else:
            scale = row_scale[2 + 2 * piece + half, rows_at(c)]
        for k in range(TILES):
            if m == 0:
                column = col_scale_wi[pl.ds(piece * TILES + k, 1)]
            else:
                column = col_scale_wo[k : k + 1]
            result = (value[:, k * LANES : (k + 1) * LANES] * scale * column).astype(jnp.bfloat16)
            if m == 0:
                update_wi[rows, pl.ds(pl.multiple_of(piece * WIDE + k * LANES, LANES), LANES)] = result
            else:
                update_wo[
                    pl.ds(pl.multiple_of(piece * PIECE + half * HALF + c * ROWS, ROWS), ROWS),
                    k * LANES : (k + 1) * LANES,
                ] = result

    for m in range(2):

        @pl.loop(0, CHUNKS)
        def _(c):
            for half in range(2):
                finish(me, m, half, c)

    for m in range(2):

        @pl.loop(0, CHUNKS)
        def _(c):
            for way in (FORWARD, BACKWARD):
                finish(target[1 - way], m, way, c)

    for m in range(2):

        @pl.loop(0, CHUNKS)
        def _(c):
            for way in (FORWARD, BACKWARD):
                source, half = target[1 - way], 1 - way
                part = total.at[source, m, pl.ds(pl.multiple_of(half * HALF + c * ROWS, ROWS), ROWS)]
                send(part, part, big_send.at[3], gather_recv.at[way, m, half, c], right).wait_recv()
                finish(source, m, half, c)

    for m in range(2):

        @pl.loop(0, CHUNKS)
        def _(c):
            for way in (FORWARD, BACKWARD):
                part = total.at[across, m, pl.ds(pl.multiple_of(way * HALF + c * ROWS, ROWS), ROWS)]
                send(part, part, big_send.at[5], onward_recv.at[way, m, c], right).wait_recv()
                finish(across, m, way, c)

    for at in range(6):
        pltpu.make_async_copy(passing, passing, big_send.at[at]).wait()


def local(n_row, n_col, grad_wi, grad_wo, row_wi, col_wi, row_wo, col_wo):
    vmem = pl.BlockSpec(memory_space=pltpu.VMEM)
    hbm = pl.BlockSpec(memory_space=pltpu.HBM)
    f32, bf16 = jnp.float32, jnp.bfloat16

    def folded(x):
        return x.reshape(x.shape[0] // LANES, LANES)

    vectors = [folded(x) for x in (row_wi, col_wi, row_wo, col_wo)]
    out = pl.pallas_call(
        functools.partial(kernel, n_row, n_col),
        out_shape=(
            jax.ShapeDtypeStruct(grad_wi.shape[1:], bf16),
            jax.ShapeDtypeStruct(vectors[0].shape, f32),
            jax.ShapeDtypeStruct(vectors[1].shape, f32),
            jax.ShapeDtypeStruct(grad_wo.shape[1:], bf16),
            jax.ShapeDtypeStruct(vectors[2].shape, f32),
            jax.ShapeDtypeStruct(vectors[3].shape, f32),
        ),
        in_specs=[hbm] * 2 + [vmem] * 4,
        out_specs=[vmem] * 6,
        scratch_shapes=[
            pltpu.VMEM((2, PIECE, WIDE), bf16),
            pltpu.VMEM((2, 2, HALF, WIDE), bf16),
            pltpu.VMEM((2, 2, HALF, WIDE), bf16),
            pltpu.VMEM((2, 2, HALF, WIDE), bf16),
            pltpu.VMEM((2, 2, HALF, WIDE), bf16),
            pltpu.VMEM((N_DP, 2, PIECE, WIDE), bf16),
            pltpu.VMEM((2, PIECE, WIDE), f32),
            pltpu.VMEM((2, PIECE, LANES), f32),
            pltpu.VMEM((2, 8, WIDE), f32),
            pltpu.VMEM((n_col, 4, LANES), f32),
            pltpu.VMEM((n_row, 8, LANES), f32),
            pltpu.VMEM((N_DP, 16, LANES), f32),
            pltpu.VMEM((2 + 2 * N_DP, LANES, LANES), f32),
            pltpu.VMEM(vectors[1].shape, f32),
            pltpu.VMEM(vectors[3].shape, f32),
            pltpu.VMEM((n_col, 2, LANES), f32),
            pltpu.VMEM((n_row, 2, LANES), f32),
            pltpu.VMEM((N_DP, 2, LANES), f32),
            pltpu.SemaphoreType.DMA((6,)),
            pltpu.SemaphoreType.DMA((6,)),
            pltpu.SemaphoreType.DMA((2, 2, CHUNKS)),
            pltpu.SemaphoreType.DMA((2, 2, CHUNKS)),
            pltpu.SemaphoreType.DMA((2, 2, CHUNKS)),
            pltpu.SemaphoreType.DMA((2, 2, 2, CHUNKS)),
            pltpu.SemaphoreType.DMA((2, 2, CHUNKS)),
            pltpu.SemaphoreType.DMA((6,)),
            pltpu.SemaphoreType.DMA((6,)),
        ],
        compiler_params=pltpu.CompilerParams(
            collective_id=0, has_side_effects=True, vmem_limit_bytes=40 * 1024 * 1024
        ),
        name="adafactor",
    )(grad_wi, grad_wo, *vectors)
    return (
        out[0],
        out[1].reshape(row_wi.shape),
        out[2].reshape(col_wi.shape),
        out[3],
        out[4].reshape(row_wo.shape),
        out[5].reshape(col_wo.shape),
    )


def solution(mesh):
    return jax.shard_map(
        functools.partial(local, mesh.shape["row"], mesh.shape["col"]),
        mesh=mesh,
        in_specs=(
            P("dp", "row", "col"),
            P("dp", "row", "col"),
            P("row"),
            P("col"),
            P("row"),
            P("col"),
        ),
        out_specs=(P("row", "col"), P("row"), P("col"), P("row", "col"), P("row"), P("col")),
        check_vma=False,
    )
```

```python
import functools

import jax
import jax.numpy as jnp
from jax import lax
from jax.experimental import pallas as pl
from jax.experimental.pallas import tpu as pltpu
from jax.sharding import PartitionSpec as P

BETA = 0.8
EPS_SQUARE = 1e-30
N_DP = 4
HALF = 128
PIECE = 2 * HALF
WIDE = 512
LANES = 128
TILES = WIDE // LANES
ROWS = 64
CHUNKS = HALF // ROWS

VMEM_LIMIT = 60 * 1024 * 1024

MESH = pl.DeviceIdType.MESH
FORWARD, BACKWARD = 0, 1


def kernel(
    n_row,
    n_col,
    grad_wi,
    grad_wo,
    row_wi_hbm,
    col_wi_hbm,
    row_wo_hbm,
    col_wo_hbm,
    update_wi,
    row_wi_new,
    col_wi_new,
    update_wo,
    row_wo_new,
    col_wo_new,
    row_wi,
    col_wi,
    row_wo,
    col_wo,
    own,
    near,
    passing,
    direct,
    combined,
    total,
    squares,
    row_part,
    col_part,
    y_one,
    z_one,
    z_two,
    x_one,
    y_two,
    x_two,
    y_energy,
    z_energy,
    row_scale,
    col_scale_wi,
    col_scale_wo,
    load_sem,
    big_send,
    passing_recv,
    direct_recv,
    combined_recv,
    gather_recv,
    onward_recv,
    small_send,
    small_recv,
):
    me = lax.axis_index("dp")
    my_row = lax.axis_index("row")
    my_col = lax.axis_index("col")
    right = lax.rem(me + 1, N_DP)
    left = lax.rem(me + N_DP - 1, N_DP)
    across = lax.rem(me + 2, N_DP)
    target = (right, left)

    def rows_at(c):
        return pl.ds(pl.multiple_of(c * ROWS, ROWS), ROWS)

    def grad_at(m, piece, start, size):
        if m == 0:
            return grad_wi.at[
                0, pl.ds(start, size), pl.ds(pl.multiple_of(piece * WIDE, WIDE), WIDE)
            ]
        return grad_wo.at[
            0, pl.ds(pl.multiple_of(piece * PIECE + start, ROWS), size), :
        ]

    def grad_chunk(m, piece, half, c):
        return grad_at(m, piece, pl.multiple_of(half * HALF + c * ROWS, ROWS), ROWS)

    loads = []
    for m in range(2):
        loads.append(pltpu.make_async_copy(grad_at(m, right, 0, HALF), near.at[FORWARD, m], load_sem.at[m]))
        loads.append(pltpu.make_async_copy(grad_at(m, left, HALF, HALF), near.at[BACKWARD, m], load_sem.at[2 + m]))
        loads.append(pltpu.make_async_copy(grad_at(m, me, 0, PIECE), own.at[m], load_sem.at[4 + m]))
    vectors = ((row_wi_hbm, row_wi), (col_wi_hbm, col_wi), (row_wo_hbm, row_wo), (col_wo_hbm, col_wo))
    for at, (source, target_ref) in enumerate(vectors):
        loads.append(pltpu.make_async_copy(source, target_ref, load_sem.at[6 + at]))
    for load in loads:
        load.start()

    barrier = pltpu.get_barrier_semaphore()

    def greet(axis, n, index):
        def body(j, carry):
            step = (j + 1) // 2
            d = n // 2 + step - 2 * step * lax.rem(j, 2)
            pl.semaphore_signal(
                barrier, inc=1, device_id={axis: lax.rem(index + d, n)}, device_id_type=MESH
            )
            return carry

        lax.fori_loop(0, n - 1, body, 0)

    greet("dp", N_DP, me)
    greet("row", n_row, my_row)
    greet("col", n_col, my_col)
    pl.semaphore_wait(barrier, N_DP + n_row + n_col - 3)

    def send(src, dst, send_sem, recv_sem, to):
        return pltpu.make_async_remote_copy(
            src_ref=src,
            dst_ref=dst,
            send_sem=send_sem,
            recv_sem=recv_sem,
            device_id={"dp": to},
            device_id_type=MESH,
        )

    def send_across(m):
        @pl.loop(0, CHUNKS)
        def _(c):
            for way in (FORWARD, BACKWARD):
                send(
                    grad_chunk(m, across, way, c),
                    passing.at[way, m, rows_at(c)],
                    big_send.at[0, m],
                    passing_recv.at[way, m, c],
                    target[way],
                ).start()

    def send_direct(m):
        @pl.loop(0, CHUNKS)
        def _(c):
            for way in (FORWARD, BACKWARD):
                send(
                    grad_chunk(m, target[way], 1 - way, c),
                    direct.at[way, m, rows_at(c)],
                    big_send.at[1, m],
                    direct_recv.at[way, m, c],
                    target[way],
                ).start()

    def send_combined(m):
        @pl.loop(0, CHUNKS)
        def _(c):
            for way in (FORWARD, BACKWARD):
                here = passing.at[way, m, rows_at(c)]
                send(here, here, big_send.at[0, m], passing_recv.at[way, m, c], target[way]).wait_recv()
                here[...] = (
                    here[...].astype(jnp.float32) + near[way, m, rows_at(c)].astype(jnp.float32)
                ).astype(jnp.bfloat16)
                send(
                    here,
                    combined.at[way, m, rows_at(c)],
                    big_send.at[2, m],
                    combined_recv.at[way, m, c],
                    target[way],
                ).start()

    send_across(0)
    send_direct(0)
    send_across(1)
    for load in loads:
        load.wait()
    send_combined(0)
    send_direct(1)
    send_combined(1)

    def gather(m, half, c, way):
        part = total.at[me, m, pl.ds(pl.multiple_of(half * HALF + c * ROWS, ROWS), ROWS)]
        return send(part, part, big_send.at[3 + half, m], gather_recv.at[way, m, half, c], target[way])

    def gather_start(m):
        for second in (0, 1):

            @pl.loop(0, CHUNKS)
            def _(c):
                for way in (FORWARD, BACKWARD):
                    half = 1 - way if second else way
                    gather(m, half, c, way).start()

    def own_totals(m):
        col_part[m] = jnp.zeros((8, WIDE), jnp.float32)

        @pl.loop(0, CHUNKS)
        def _(c):
            for way in (FORWARD, BACKWARD):
                first = direct.at[1 - way, m, rows_at(c)]
                second = combined.at[way, m, rows_at(c)]
                send(first, first, big_send.at[1, m], direct_recv.at[1 - way, m, c], right).wait_recv()
                send(second, second, big_send.at[2, m], combined_recv.at[way, m, c], right).wait_recv()
                rows = pl.ds(pl.multiple_of(way * HALF + c * ROWS, ROWS), ROWS)
                value = (
                    own[m, rows].astype(jnp.float32)
                    + first[...].astype(jnp.float32)
                    + second[...].astype(jnp.float32)
                )
                total[me, m, rows] = value.astype(jnp.bfloat16)
                square = value * value
                squares[m, rows] = square
                row_part[m, rows] = sum(
                    square[:, k * LANES : (k + 1) * LANES] for k in range(TILES)
                )
                col_part[m] += jnp.sum(square.reshape(ROWS // 8, 8, WIDE), axis=0)

    def exchange_start(buffer, n, axis, index, at):
        def body(j, carry):
            step = (j + 1) // 2
            d = n // 2 + step - 2 * step * lax.rem(j, 2)
            pltpu.make_async_remote_copy(
                src_ref=buffer.at[index],
                dst_ref=buffer.at[index],
                send_sem=small_send.at[at],
                recv_sem=small_recv.at[at],
                device_id={axis: lax.rem(index + d, n)},
                device_id_type=MESH,
            ).start()
            return carry

        lax.fori_loop(0, n - 1, body, 0)

    def exchange_wait(buffer, n, axis, index, at):
        others = buffer.at[pl.ds(0, n - 1)]
        pltpu.make_async_copy(others, others, small_recv.at[at]).wait()
        pltpu.make_async_copy(others, others, small_send.at[at]).wait()

    def over_col(buffer, at):
        return buffer, n_col, "col", my_col, at

    def over_row(buffer, at):
        return buffer, n_row, "row", my_row, at

    def over_dp(buffer, at):
        return buffer, N_DP, "dp", me, at

    def add_up(buffer, n):
        result = buffer[0]
        for j in range(1, n):
            result = result + buffer[j]
        return result

    def mix(previous, sums, count):
        return BETA * previous + (1.0 - BETA) * (sums * (1.0 / count) + EPS_SQUARE)

    def down(x):
        return jnp.broadcast_to(x, (LANES, LANES)).T

    def fold_rows(part):
        halves = [part[half * HALF : (half + 1) * HALF].T for half in range(2)]
        return jnp.concatenate([jnp.sum(x, axis=0, keepdims=True) for x in halves], axis=0)

    def row_sums(m):
        return fold_rows(row_part[m])

    def col_sums(m):
        column = jnp.sum(col_part[m], axis=0, keepdims=True)
        return jnp.concatenate([column[:, k * LANES : (k + 1) * LANES] for k in range(TILES)], axis=0)

    def weighted_row_sums(m, inverse):
        return fold_rows(
            sum(squares[m, :, k * LANES : (k + 1) * LANES] * inverse[k : k + 1] for k in range(TILES))
        )

    def weighted_col_sums(m, inverse):
        weights = [down(inverse[half : half + 1]) for half in range(2)]
        result = []
        for k in range(TILES):
            part = jnp.zeros((8, LANES), jnp.float32)
            for half in range(2):
                x = squares[m, half * HALF : (half + 1) * HALF, k * LANES : (k + 1) * LANES] * weights[half]
                part += jnp.sum(x.reshape(HALF // 8, 8, LANES), axis=0)
            result.append(jnp.sum(part, axis=0, keepdims=True))
        return jnp.concatenate(result, axis=0)

    def onward(m):
        @pl.loop(0, CHUNKS)
        def _(c):
            for way in (FORWARD, BACKWARD):
                source = target[1 - way]
                half = way
                part = total.at[source, m, pl.ds(pl.multiple_of(half * HALF + c * ROWS, ROWS), ROWS)]
                send(part, part, big_send.at[3, m], gather_recv.at[way, m, half, c], right).wait_recv()
                send(part, part, big_send.at[5, m], onward_recv.at[way, m, c], target[way]).start()

    rows_wi, rows_wo = n_row * PIECE, n_row * PIECE * N_DP
    cols_wi, cols_wo = n_col * WIDE * N_DP, n_col * WIDE

    own_totals(0)
    y_one[my_row] = col_sums(0)
    exchange_start(*over_row(y_one, 0))
    pltpu.make_async_copy(passing.at[0], passing.at[0], big_send.at[2, 1]).wait()
    gather_start(0)
    own_totals(1)
    z_one[my_col] = row_sums(1)
    exchange_start(*over_col(z_one, 1))
    gather_start(1)

    exchange_wait(*over_row(y_one, 0))
    col_sums_wi = add_up(y_one, n_row)
    own_col_wi = mix(col_wi[pl.ds(me * TILES, TILES)], col_sums_wi, rows_wi)
    z_two[my_col] = jnp.concatenate(
        [row_sums(0), weighted_row_sums(0, 1.0 / own_col_wi)], axis=0
    )
    exchange_start(*over_col(z_two, 2))
    x_one[me] = col_sums_wi
    exchange_start(*over_dp(x_one, 3))
    y_two[my_row, 0:4] = col_sums(1)
    exchange_wait(*over_col(z_one, 1))
    row_sums_wo = add_up(z_one, n_col)
    own_row_wo = mix(row_wo[pl.ds(me * 2, 2)], row_sums_wo, cols_wo)
    y_two[my_row, 4:8] = weighted_col_sums(1, 1.0 / own_row_wo)
    exchange_start(*over_row(y_two, 4))
    exchange_wait(*over_col(z_two, 2))
    x_two[me, 8:12] = add_up(z_two, n_col)
    x_two[me, 12:14] = row_sums_wo
    x_two[me, 14:16] = row_sums_wo
    exchange_wait(*over_row(y_two, 4))
    x_two[me, 0:8] = add_up(y_two, n_row)
    exchange_start(*over_dp(x_two, 5))
    onward(0)
    onward(1)
    exchange_wait(*over_dp(x_two, 5))
    sums = add_up(x_two, N_DP)

    new_row_wi = mix(row_wi[...], sums[8:10], cols_wi)
    energy = jnp.sum(sums[10:12] / new_row_wi, axis=0, keepdims=True)
    y_energy[my_row] = jnp.concatenate([energy, energy], axis=0)
    exchange_start(*over_row(y_energy, 6))
    new_col_wo = mix(col_wo[...], sums[0:4], rows_wo)
    energy = jnp.sum(sums[4:8] / new_col_wo, axis=0, keepdims=True)
    z_energy[my_col] = jnp.concatenate([energy, energy], axis=0)
    exchange_start(*over_col(z_energy, 7))

    row_wi_new[...] = new_row_wi
    factor = lax.rsqrt(new_row_wi)
    for half in range(2):
        row_scale[half] = down(factor[half : half + 1])
    new = mix(row_wo[...], jnp.concatenate([x_two[x, 12:14] for x in range(N_DP)], axis=0), cols_wo)
    row_wo_new[...] = new
    factor = lax.rsqrt(new)
    for half in range(2 * N_DP):
        row_scale[2 + half] = down(factor[half : half + 1])
    exchange_wait(*over_dp(x_one, 3))
    new = mix(col_wi[...], jnp.concatenate([x_one[x] for x in range(N_DP)], axis=0), rows_wi)
    col_wi_new[...] = new
    factor_wi = lax.rsqrt(new)
    col_wo_new[...] = new_col_wo
    factor_wo = lax.rsqrt(new_col_wo)

    def clip(sums):
        energy = jnp.sum(sums[0:1], axis=1, keepdims=True)
        return 1.0 / jnp.maximum(1.0, jnp.sqrt(energy * (1.0 / (rows_wi * cols_wi))))

    exchange_wait(*over_col(z_energy, 7))
    col_scale_wo[...] = factor_wo * clip(add_up(z_energy, n_col))
    exchange_wait(*over_row(y_energy, 6))
    col_scale_wi[...] = factor_wi * clip(add_up(y_energy, n_row))

    def finish(piece, m, half, c):
        rows = pl.ds(pl.multiple_of(half * HALF + c * ROWS, ROWS), ROWS)
        value = total[piece, m, rows].astype(jnp.float32)
        if m == 0:
            scale = row_scale[half, rows_at(c)]
        else:
            scale = row_scale[2 + 2 * piece + half, rows_at(c)]
        for k in range(TILES):
            if m == 0:
                column = col_scale_wi[pl.ds(piece * TILES + k, 1)]
            else:
                column = col_scale_wo[k : k + 1]
            result = (value[:, k * LANES : (k + 1) * LANES] * scale * column).astype(jnp.bfloat16)
            if m == 0:
                update_wi[rows, pl.ds(pl.multiple_of(piece * WIDE + k * LANES, LANES), LANES)] = result
            else:
                update_wo[
                    pl.ds(pl.multiple_of(piece * PIECE + half * HALF + c * ROWS, ROWS), ROWS),
                    k * LANES : (k + 1) * LANES,
                ] = result

    for m in range(2):

        @pl.loop(0, CHUNKS)
        def _(c):
            for half in range(2):
                finish(me, m, half, c)

    for m in range(2):

        @pl.loop(0, CHUNKS)
        def _(c):
            for way in (FORWARD, BACKWARD):
                finish(target[1 - way], m, way, c)

    for m in range(2):

        @pl.loop(0, CHUNKS)
        def _(c):
            for way in (FORWARD, BACKWARD):
                source, half = target[1 - way], 1 - way
                part = total.at[source, m, pl.ds(pl.multiple_of(half * HALF + c * ROWS, ROWS), ROWS)]
                send(part, part, big_send.at[3, m], gather_recv.at[way, m, half, c], right).wait_recv()
                finish(source, m, half, c)

    for m in range(2):

        @pl.loop(0, CHUNKS)
        def _(c):
            for way in (FORWARD, BACKWARD):
                part = total.at[across, m, pl.ds(pl.multiple_of(way * HALF + c * ROWS, ROWS), ROWS)]
                send(part, part, big_send.at[5, m], onward_recv.at[way, m, c], right).wait_recv()
                finish(across, m, way, c)

    for at in range(6):
        for m in range(2):
            if (at, m) != (2, 1):
                pltpu.make_async_copy(passing.at[0], passing.at[0], big_send.at[at, m]).wait()


def write_back(*refs):
    sources, results, sem = refs[:6], refs[6:12], refs[12]
    copies = [pltpu.make_async_copy(a, b, sem.at[i]) for i, (a, b) in enumerate(zip(sources, results))]
    for copy in copies:
        copy.start()
    for copy in copies:
        copy.wait()


def local(n_row, n_col, grad_wi, grad_wo, row_wi, col_wi, row_wo, col_wo):
    vmem = pl.BlockSpec(memory_space=pltpu.VMEM)
    hbm = pl.BlockSpec(memory_space=pltpu.HBM)
    f32, bf16 = jnp.float32, jnp.bfloat16

    def folded(x):
        return x.reshape(x.shape[0] // LANES, LANES)

    vectors = [folded(x) for x in (row_wi, col_wi, row_wo, col_wo)]
    out = pl.pallas_call(
        functools.partial(kernel, n_row, n_col),
        out_shape=(
            pltpu.VMEM(grad_wi.shape[1:], bf16),
            pltpu.VMEM(vectors[0].shape, f32),
            pltpu.VMEM(vectors[1].shape, f32),
            pltpu.VMEM(grad_wo.shape[1:], bf16),
            pltpu.VMEM(vectors[2].shape, f32),
            pltpu.VMEM(vectors[3].shape, f32),
        ),
        in_specs=[hbm] * 6,
        out_specs=[vmem] * 6,
        scratch_shapes=[pltpu.VMEM(x.shape, f32) for x in vectors]
        + [
            pltpu.VMEM((2, PIECE, WIDE), bf16),
            pltpu.VMEM((2, 2, HALF, WIDE), bf16),
            pltpu.VMEM((2, 2, HALF, WIDE), bf16),
            pltpu.VMEM((2, 2, HALF, WIDE), bf16),
            pltpu.VMEM((2, 2, HALF, WIDE), bf16),
            pltpu.VMEM((N_DP, 2, PIECE, WIDE), bf16),
            pltpu.VMEM((2, PIECE, WIDE), f32),
            pltpu.VMEM((2, PIECE, LANES), f32),
            pltpu.VMEM((2, 8, WIDE), f32),
            pltpu.VMEM((n_row, 4, LANES), f32),
            pltpu.VMEM((n_col, 2, LANES), f32),
            pltpu.VMEM((n_col, 4, LANES), f32),
            pltpu.VMEM((N_DP, 4, LANES), f32),
            pltpu.VMEM((n_row, 8, LANES), f32),
            pltpu.VMEM((N_DP, 16, LANES), f32),
            pltpu.VMEM((n_row, 2, LANES), f32),
            pltpu.VMEM((n_col, 2, LANES), f32),
            pltpu.VMEM((2 + 2 * N_DP, LANES, LANES), f32),
            pltpu.VMEM(vectors[1].shape, f32),
            pltpu.VMEM(vectors[3].shape, f32),
            pltpu.SemaphoreType.DMA((10,)),
            pltpu.SemaphoreType.DMA((6, 2)),
            pltpu.SemaphoreType.DMA((2, 2, CHUNKS)),
            pltpu.SemaphoreType.DMA((2, 2, CHUNKS)),
            pltpu.SemaphoreType.DMA((2, 2, CHUNKS)),
            pltpu.SemaphoreType.DMA((2, 2, 2, CHUNKS)),
            pltpu.SemaphoreType.DMA((2, 2, CHUNKS)),
            pltpu.SemaphoreType.DMA((8,)),
            pltpu.SemaphoreType.DMA((8,)),
        ],
        compiler_params=pltpu.CompilerParams(
            collective_id=0, has_side_effects=True, vmem_limit_bytes=VMEM_LIMIT
        ),
        name="adafactor",
    )(grad_wi, grad_wo, *vectors)
    out = pl.pallas_call(
        write_back,
        out_shape=tuple(jax.ShapeDtypeStruct(x.shape, x.dtype) for x in out),
        in_specs=[vmem] * 6,
        out_specs=[hbm] * 6,
        scratch_shapes=[pltpu.SemaphoreType.DMA((6,))],
        compiler_params=pltpu.CompilerParams(vmem_limit_bytes=2 * 1024 * 1024),
        name="write_back",
    )(*[pltpu.with_memory_space_constraint(x, pltpu.VMEM) for x in out])
    return (
        out[0],
        out[1].reshape(row_wi.shape),
        out[2].reshape(col_wi.shape),
        out[3],
        out[4].reshape(row_wo.shape),
        out[5].reshape(col_wo.shape),
    )


def solution(mesh):
    return jax.shard_map(
        functools.partial(local, mesh.shape["row"], mesh.shape["col"]),
        mesh=mesh,
        in_specs=(
            P("dp", "row", "col"),
            P("dp", "row", "col"),
            P("row"),
            P("col"),
            P("row"),
            P("col"),
        ),
        out_specs=(P("row", "col"), P("row"), P("col"), P("row", "col"), P("row"), P("col")),
        check_vma=False,
    )
```

```python
import functools

import jax
import jax.numpy as jnp
from jax import lax
from jax.experimental import pallas as pl
from jax.experimental.pallas import tpu as pltpu
from jax.sharding import PartitionSpec as P

BETA = 0.8
EPS_SQUARE = 1e-30
N_DP = 4
HALF = 128
PIECE = 2 * HALF
WIDE = 512
LANES = 128
TILES = WIDE // LANES
ROWS = 128
CHUNKS = HALF // ROWS

VMEM_LIMIT = 60 * 1024 * 1024

MESH = pl.DeviceIdType.MESH
FORWARD, BACKWARD = 0, 1


def kernel(
    n_row,
    n_col,
    grad_wi,
    grad_wo,
    row_wi_hbm,
    col_wi_hbm,
    row_wo_hbm,
    col_wo_hbm,
    total,
    row_scale,
    col_scale_wi,
    col_scale_wo,
    row_wi_new,
    col_wi_new,
    row_wo_new,
    col_wo_new,
    row_wi,
    col_wi,
    row_wo,
    col_wo,
    own,
    near,
    passing,
    direct,
    combined,
    squares,
    row_part,
    col_part,
    y_one,
    z_one,
    z_two,
    x_one,
    y_two,
    x_two,
    x_three,
    y_energy,
    z_energy,
    ready,
    load_sem,
    big_send,
    passing_recv,
    direct_recv,
    combined_recv,
    gather_recv,
    onward_recv,
    small_send,
    small_recv,
):
    me = lax.axis_index("dp")
    my_row = lax.axis_index("row")
    my_col = lax.axis_index("col")
    right = lax.rem(me + 1, N_DP)
    left = lax.rem(me + N_DP - 1, N_DP)
    across = lax.rem(me + 2, N_DP)
    target = (right, left)

    def rows_at(c):
        return pl.ds(pl.multiple_of(c * ROWS, ROWS), ROWS)

    def grad_at(m, piece, start, size):
        if m == 0:
            return grad_wi.at[
                0, pl.ds(start, size), pl.ds(pl.multiple_of(piece * WIDE, WIDE), WIDE)
            ]
        return grad_wo.at[
            0, pl.ds(pl.multiple_of(piece * PIECE + start, ROWS), size), :
        ]

    def grad_chunk(m, piece, half, c):
        return grad_at(m, piece, pl.multiple_of(half * HALF + c * ROWS, ROWS), ROWS)

    loads = []
    for m in range(2):
        loads.append(pltpu.make_async_copy(grad_at(m, right, 0, HALF), near.at[FORWARD, m], load_sem.at[m]))
        loads.append(pltpu.make_async_copy(grad_at(m, left, HALF, HALF), near.at[BACKWARD, m], load_sem.at[2 + m]))
        loads.append(pltpu.make_async_copy(grad_at(m, me, 0, PIECE), own.at[m], load_sem.at[4 + m]))
    vectors = ((row_wi_hbm, row_wi), (col_wi_hbm, col_wi), (row_wo_hbm, row_wo), (col_wo_hbm, col_wo))
    for at, (source, target_ref) in enumerate(vectors):
        loads.append(pltpu.make_async_copy(source, target_ref, load_sem.at[6 + at]))
    for load in loads:
        load.start()

    barrier = pltpu.get_barrier_semaphore()

    n_y = n_row // 2
    core = lax.rem(my_row, 2)

    def beside(n):
        return [] if n == 1 else [1] if n == 2 else [1, n - 1]

    def signal(sem, axis, n, index, d):
        pl.semaphore_signal(
            sem, inc=1, device_id={axis: lax.rem(index + d, n)}, device_id_type=MESH
        )

    near_row = [2 * d for d in beside(n_y)]
    near_col = beside(n_col)
    for d in range(1, N_DP):
        signal(barrier, "dp", N_DP, me, d)
    for d in near_row:
        signal(barrier, "row", n_row, my_row, d)
    for d in near_col:
        signal(barrier, "col", n_col, my_col, d)
    pl.semaphore_signal(barrier, inc=1, device_id={"row": my_row + 1 - 2 * core}, device_id_type=MESH)
    pl.semaphore_wait(barrier, N_DP + len(near_row) + len(near_col))

    def tell(at):
        for d in near_row:
            signal(ready.at[0, at], "row", n_row, my_row, d)
        for d in near_col:
            signal(ready.at[1, at], "col", n_col, my_col, d)

    def hear(at):
        for axis, count in ((0, len(near_row)), (1, len(near_col))):
            if count:
                pl.semaphore_wait(ready.at[axis, at], count)

    def send(src, dst, send_sem, recv_sem, to):
        return pltpu.make_async_remote_copy(
            src_ref=src,
            dst_ref=dst,
            send_sem=send_sem,
            recv_sem=recv_sem,
            device_id={"dp": to},
            device_id_type=MESH,
        )

    def send_across(m):
        @pl.loop(0, CHUNKS)
        def _(c):
            for way in (FORWARD, BACKWARD):
                send(
                    grad_chunk(m, across, way, c),
                    passing.at[way, m, rows_at(c)],
                    big_send.at[0, m],
                    passing_recv.at[way, m, c],
                    target[way],
                ).start()

    def send_direct(m):
        @pl.loop(0, CHUNKS)
        def _(c):
            for way in (FORWARD, BACKWARD):
                send(
                    grad_chunk(m, target[way], 1 - way, c),
                    direct.at[way, m, rows_at(c)],
                    big_send.at[1, m],
                    direct_recv.at[way, m, c],
                    target[way],
                ).start()

    def send_combined(m):
        @pl.loop(0, CHUNKS)
        def _(c):
            for way in (FORWARD, BACKWARD):
                here = passing.at[way, m, rows_at(c)]
                send(here, here, big_send.at[0, m], passing_recv.at[way, m, c], target[way]).wait_recv()
                here[...] = (
                    here[...].astype(jnp.float32) + near[way, m, rows_at(c)].astype(jnp.float32)
                ).astype(jnp.bfloat16)
                send(
                    here,
                    combined.at[way, m, rows_at(c)],
                    big_send.at[2, m],
                    combined_recv.at[way, m, c],
                    target[way],
                ).start()

    send_across(0)
    send_direct(0)
    send_across(1)
    tell(0)
    for load in loads:
        load.wait()
    hear(0)
    tell(1)
    send_combined(0)
    send_direct(1)
    hear(1)
    tell(2)
    send_combined(1)
    hear(2)
    tell(3)

    def gather(m, half, c, way):
        part = total.at[me, m, pl.ds(pl.multiple_of(half * HALF + c * ROWS, ROWS), ROWS)]
        return send(part, part, big_send.at[3 + half, m], gather_recv.at[way, m, half, c], target[way])

    def gather_start(m):
        for second in (0, 1):

            @pl.loop(0, CHUNKS)
            def _(c):
                for way in (FORWARD, BACKWARD):
                    half = 1 - way if second else way
                    gather(m, half, c, way).start()

    def own_totals(m):
        col_part[m] = jnp.zeros((8, WIDE), jnp.float32)

        @pl.loop(0, CHUNKS)
        def _(c):
            for way in (FORWARD, BACKWARD):
                first = direct.at[1 - way, m, rows_at(c)]
                second = combined.at[way, m, rows_at(c)]
                send(first, first, big_send.at[1, m], direct_recv.at[1 - way, m, c], right).wait_recv()
                send(second, second, big_send.at[2, m], combined_recv.at[way, m, c], right).wait_recv()
                rows = pl.ds(pl.multiple_of(way * HALF + c * ROWS, ROWS), ROWS)
                value = (
                    own[m, rows].astype(jnp.float32)
                    + first[...].astype(jnp.float32)
                    + second[...].astype(jnp.float32)
                )
                total[me, m, rows] = value.astype(jnp.bfloat16)
                square = value * value
                squares[m, rows] = square
                row_part[m, rows] = sum(
                    square[:, k * LANES : (k + 1) * LANES] for k in range(TILES)
                )
                col_part[m] += jnp.sum(square.reshape(ROWS // 8, 8, WIDE), axis=0)

    def exchange_start(buffer, n, axis, index, at):
        def body(j, carry):
            step = (j + 1) // 2
            d = n // 2 + step - 2 * step * lax.rem(j, 2)
            pltpu.make_async_remote_copy(
                src_ref=buffer.at[index],
                dst_ref=buffer.at[index],
                send_sem=small_send.at[at],
                recv_sem=small_recv.at[at],
                device_id={axis: lax.rem(index + d, n)},
                device_id_type=MESH,
            ).start()
            return carry

        lax.fori_loop(0, n - 1, body, 0)

    def exchange_wait(buffer, n, axis, index, at):
        others = buffer.at[pl.ds(0, n - 1)]
        pltpu.make_async_copy(others, others, small_recv.at[at]).wait()
        pltpu.make_async_copy(others, others, small_send.at[at]).wait()

    def over_col(buffer, at):
        return buffer, n_col, "col", my_col, at

    def over_row(buffer, at):
        return buffer, n_row, "row", my_row, at

    def over_dp(buffer, at):
        return buffer, N_DP, "dp", me, at

    def add_up(buffer, n):
        result = buffer[0]
        for j in range(1, n):
            result = result + buffer[j]
        return result

    def mix(previous, sums, count):
        return BETA * previous + (1.0 - BETA) * (sums * (1.0 / count) + EPS_SQUARE)

    def down(x):
        return jnp.broadcast_to(x, (LANES, LANES)).T

    def fold_rows(part):
        halves = [part[half * HALF : (half + 1) * HALF].T for half in range(2)]
        return jnp.concatenate([jnp.sum(x, axis=0, keepdims=True) for x in halves], axis=0)

    def row_sums(m):
        return fold_rows(row_part[m])

    def col_sums(m):
        column = jnp.sum(col_part[m], axis=0, keepdims=True)
        return jnp.concatenate([column[:, k * LANES : (k + 1) * LANES] for k in range(TILES)], axis=0)

    def weighted_row_sums(m, inverse):
        return fold_rows(
            sum(squares[m, :, k * LANES : (k + 1) * LANES] * inverse[k : k + 1] for k in range(TILES))
        )

    def weighted_col_sums(m, inverse):
        weights = [down(inverse[half : half + 1]) for half in range(2)]
        result = []
        for k in range(TILES):
            part = jnp.zeros((8, LANES), jnp.float32)
            for half in range(2):
                x = squares[m, half * HALF : (half + 1) * HALF, k * LANES : (k + 1) * LANES] * weights[half]
                part += jnp.sum(x.reshape(HALF // 8, 8, LANES), axis=0)
            result.append(jnp.sum(part, axis=0, keepdims=True))
        return jnp.concatenate(result, axis=0)

    def onward(m):
        @pl.loop(0, CHUNKS)
        def _(c):
            for way in (FORWARD, BACKWARD):
                source = target[1 - way]
                half = way
                part = total.at[source, m, pl.ds(pl.multiple_of(half * HALF + c * ROWS, ROWS), ROWS)]
                send(part, part, big_send.at[3, m], gather_recv.at[way, m, half, c], right).wait_recv()
                send(part, part, big_send.at[5, m], onward_recv.at[way, m, c], target[way]).start()

    rows_wi, rows_wo = n_row * PIECE, n_row * PIECE * N_DP
    cols_wi, cols_wo = n_col * WIDE * N_DP, n_col * WIDE

    own_totals(0)
    hear(3)
    y_one[my_row] = col_sums(0)
    exchange_start(*over_row(y_one, 0))
    pltpu.make_async_copy(passing.at[0], passing.at[0], big_send.at[2, 1]).wait()
    gather_start(0)
    own_totals(1)
    z_one[my_col] = row_sums(1)
    exchange_start(*over_col(z_one, 1))
    gather_start(1)

    exchange_wait(*over_row(y_one, 0))
    col_sums_wi = add_up(y_one, n_row)
    own_col_wi = mix(col_wi[pl.ds(me * TILES, TILES)], col_sums_wi, rows_wi)
    z_two[my_col] = jnp.concatenate(
        [row_sums(0), weighted_row_sums(0, 1.0 / own_col_wi)], axis=0
    )
    exchange_start(*over_col(z_two, 2))
    y_two[my_row, 0:4] = col_sums(1)
    exchange_wait(*over_col(z_one, 1))
    row_sums_wo = add_up(z_one, n_col)
    own_row_wo = mix(row_wo[pl.ds(me * 2, 2)], row_sums_wo, cols_wo)
    y_two[my_row, 4:8] = weighted_col_sums(1, 1.0 / own_row_wo)
    exchange_start(*over_row(y_two, 4))

    exchange_wait(*over_col(z_two, 2))
    x_one[me] = jnp.concatenate([add_up(z_two, n_col), col_sums_wi], axis=0)
    exchange_start(*over_dp(x_one, 3))
    exchange_wait(*over_row(y_two, 4))
    x_two[me] = add_up(y_two, n_row)
    exchange_start(*over_dp(x_two, 5))
    x_three[me] = row_sums_wo
    exchange_start(*over_dp(x_three, 8))
    onward(0)
    onward(1)
    exchange_wait(*over_dp(x_one, 3))
    sums = x_one[0, 0:4] + x_one[1, 0:4] + x_one[2, 0:4] + x_one[3, 0:4]
    new_row_wi = mix(row_wi[...], sums[0:2], cols_wi)
    energy = jnp.sum(sums[2:4] / new_row_wi, axis=0, keepdims=True)
    y_energy[my_row] = jnp.concatenate([energy, energy], axis=0)
    exchange_start(*over_row(y_energy, 6))
    exchange_wait(*over_dp(x_two, 5))
    sums = add_up(x_two, N_DP)
    new_col_wo = mix(col_wo[...], sums[0:4], rows_wo)
    energy = jnp.sum(sums[4:8] / new_col_wo, axis=0, keepdims=True)
    z_energy[my_col] = jnp.concatenate([energy, energy], axis=0)
    exchange_start(*over_col(z_energy, 7))

    row_wi_new[...] = new_row_wi
    factor = lax.rsqrt(new_row_wi)
    for half in range(2):
        row_scale[half] = down(factor[half : half + 1])
    exchange_wait(*over_dp(x_three, 8))
    new = mix(row_wo[...], jnp.concatenate([x_three[x] for x in range(N_DP)], axis=0), cols_wo)
    row_wo_new[...] = new
    factor = lax.rsqrt(new)
    for half in range(2 * N_DP):
        row_scale[2 + half] = down(factor[half : half + 1])
    new = mix(col_wi[...], jnp.concatenate([x_one[x, 4:8] for x in range(N_DP)], axis=0), rows_wi)
    col_wi_new[...] = new
    factor_wi = lax.rsqrt(new)
    col_wo_new[...] = new_col_wo
    factor_wo = lax.rsqrt(new_col_wo)

    def clip(sums):
        energy = jnp.sum(sums[0:1], axis=1, keepdims=True)
        return 1.0 / jnp.maximum(1.0, jnp.sqrt(energy * (1.0 / (rows_wi * cols_wi))))

    exchange_wait(*over_row(y_energy, 6))
    col_scale_wi[...] = factor_wi * clip(add_up(y_energy, n_row))
    exchange_wait(*over_col(z_energy, 7))
    col_scale_wo[...] = factor_wo * clip(add_up(z_energy, n_col))

    for m in range(2):

        @pl.loop(0, CHUNKS)
        def _(c):
            for way in (FORWARD, BACKWARD):
                half = 1 - way
                part = total.at[target[1 - way], m, pl.ds(pl.multiple_of(half * HALF + c * ROWS, ROWS), ROWS)]
                send(part, part, big_send.at[3, m], gather_recv.at[way, m, half, c], right).wait_recv()
                part = total.at[across, m, pl.ds(pl.multiple_of(way * HALF + c * ROWS, ROWS), ROWS)]
                send(part, part, big_send.at[5, m], onward_recv.at[way, m, c], right).wait_recv()

    for at in range(6):
        for m in range(2):
            if (at, m) != (2, 1):
                pltpu.make_async_copy(passing.at[0], passing.at[0], big_send.at[at, m]).wait()


def finish(
    total,
    row_scale,
    col_scale_wi,
    col_scale_wo,
    row_wi_new,
    col_wi_new,
    row_wo_new,
    col_wo_new,
    update_wi,
    row_wi_out,
    col_wi_out,
    update_wo,
    row_wo_out,
    col_wo_out,
    ready_wi,
    ready_wo,
    small_sem,
    big_sem,
):
    small = [
        pltpu.make_async_copy(source, result, small_sem.at[at])
        for at, (source, result) in enumerate(
            (
                (row_wi_new, row_wi_out),
                (col_wi_new, col_wi_out),
                (row_wo_new, row_wo_out),
                (col_wo_new, col_wo_out),
            )
        )
    ]
    for copy in small:
        copy.start()

    def block(m, piece, half):
        if m == 0:
            at = (
                pl.ds(pl.multiple_of(half * HALF, HALF), HALF),
                pl.ds(pl.multiple_of(piece * WIDE, WIDE), WIDE),
            )
            return ready_wi.at[at], update_wi.at[at]
        at = pl.ds(pl.multiple_of(piece * PIECE + half * HALF, HALF), HALF)
        return ready_wo.at[at], update_wo.at[at]

    def write(m, piece, half):
        source, result = block(m, piece, half)
        return pltpu.make_async_copy(source, result, big_sem.at[m, piece, half])

    for m in range(2):

        @pl.loop(0, 2 * N_DP)
        def _(step):
            piece, half = step // 2, step % 2
            ready = block(m, piece, half)[0]
            rows = pl.ds(pl.multiple_of(half * HALF, HALF), HALF)
            value = total[piece, m, rows].astype(jnp.float32)
            scale = row_scale[half] if m == 0 else row_scale[2 + step]
            for k in range(TILES):
                if m == 0:
                    column = col_scale_wi[pl.ds(piece * TILES + k, 1)]
                else:
                    column = col_scale_wo[k : k + 1]
                part = slice(k * LANES, (k + 1) * LANES)
                ready[:, part] = (value[:, part] * scale * column).astype(jnp.bfloat16)
            write(m, piece, half).start()

    for copy in small:
        copy.wait()
    for m in range(2):

        @pl.loop(0, 2 * N_DP)
        def _(step):
            write(m, step // 2, step % 2).wait()


def local(n_row, n_col, grad_wi, grad_wo, row_wi, col_wi, row_wo, col_wo):
    vmem = pl.BlockSpec(memory_space=pltpu.VMEM)
    hbm = pl.BlockSpec(memory_space=pltpu.HBM)
    f32, bf16 = jnp.float32, jnp.bfloat16

    def folded(x):
        return x.reshape(x.shape[0] // LANES, LANES)

    vectors = [folded(x) for x in (row_wi, col_wi, row_wo, col_wo)]
    out = pl.pallas_call(
        functools.partial(kernel, n_row, n_col),
        out_shape=(
            pltpu.VMEM((N_DP, 2, PIECE, WIDE), bf16),
            pltpu.VMEM((2 + 2 * N_DP, LANES, LANES), f32),
            pltpu.VMEM(vectors[1].shape, f32),
            pltpu.VMEM(vectors[3].shape, f32),
        )
        + tuple(pltpu.VMEM(x.shape, f32) for x in vectors),
        in_specs=[hbm] * 6,
        out_specs=[vmem] * 8,
        scratch_shapes=[pltpu.VMEM(x.shape, f32) for x in vectors]
        + [
            pltpu.VMEM((2, PIECE, WIDE), bf16),
            pltpu.VMEM((2, 2, HALF, WIDE), bf16),
            pltpu.VMEM((2, 2, HALF, WIDE), bf16),
            pltpu.VMEM((2, 2, HALF, WIDE), bf16),
            pltpu.VMEM((2, 2, HALF, WIDE), bf16),
            pltpu.VMEM((2, PIECE, WIDE), f32),
            pltpu.VMEM((2, PIECE, LANES), f32),
            pltpu.VMEM((2, 8, WIDE), f32),
            pltpu.VMEM((n_row, 4, LANES), f32),
            pltpu.VMEM((n_col, 2, LANES), f32),
            pltpu.VMEM((n_col, 4, LANES), f32),
            pltpu.VMEM((N_DP, 8, LANES), f32),
            pltpu.VMEM((n_row, 8, LANES), f32),
            pltpu.VMEM((N_DP, 8, LANES), f32),
            pltpu.VMEM((N_DP, 2, LANES), f32),
            pltpu.VMEM((n_row, 2, LANES), f32),
            pltpu.VMEM((n_col, 2, LANES), f32),
            pltpu.SemaphoreType.REGULAR((2, 4)),
            pltpu.SemaphoreType.DMA((10,)),
            pltpu.SemaphoreType.DMA((6, 2)),
            pltpu.SemaphoreType.DMA((2, 2, CHUNKS)),
            pltpu.SemaphoreType.DMA((2, 2, CHUNKS)),
            pltpu.SemaphoreType.DMA((2, 2, CHUNKS)),
            pltpu.SemaphoreType.DMA((2, 2, 2, CHUNKS)),
            pltpu.SemaphoreType.DMA((2, 2, CHUNKS)),
            pltpu.SemaphoreType.DMA((9,)),
            pltpu.SemaphoreType.DMA((9,)),
        ],
        compiler_params=pltpu.CompilerParams(
            collective_id=0, has_side_effects=True, vmem_limit_bytes=VMEM_LIMIT
        ),
        name="adafactor",
    )(grad_wi, grad_wo, *vectors)
    out = pl.pallas_call(
        finish,
        out_shape=(
            jax.ShapeDtypeStruct(grad_wi.shape[1:], bf16),
            jax.ShapeDtypeStruct(vectors[0].shape, f32),
            jax.ShapeDtypeStruct(vectors[1].shape, f32),
            jax.ShapeDtypeStruct(grad_wo.shape[1:], bf16),
            jax.ShapeDtypeStruct(vectors[2].shape, f32),
            jax.ShapeDtypeStruct(vectors[3].shape, f32),
        ),
        in_specs=[vmem] * 8,
        out_specs=[hbm] * 6,
        scratch_shapes=[
            pltpu.VMEM(grad_wi.shape[1:], bf16),
            pltpu.VMEM(grad_wo.shape[1:], bf16),
            pltpu.SemaphoreType.DMA((4,)),
            pltpu.SemaphoreType.DMA((2, N_DP, 2)),
        ],
        compiler_params=pltpu.CompilerParams(vmem_limit_bytes=6 * 1024 * 1024),
        name="finish",
    )(*[pltpu.with_memory_space_constraint(x, pltpu.VMEM) for x in out])
    return (
        out[0],
        out[1].reshape(row_wi.shape),
        out[2].reshape(col_wi.shape),
        out[3],
        out[4].reshape(row_wo.shape),
        out[5].reshape(col_wo.shape),
    )


def solution(mesh):
    return jax.shard_map(
        functools.partial(local, mesh.shape["row"], mesh.shape["col"]),
        mesh=mesh,
        in_specs=(
            P("dp", "row", "col"),
            P("dp", "row", "col"),
            P("row"),
            P("col"),
            P("row"),
            P("col"),
        ),
        out_specs=(P("row", "col"), P("row"), P("col"), P("row", "col"), P("row"), P("col")),
        check_vma=False,
    )
```

```python
import functools

import jax
import jax.numpy as jnp
from jax import lax
from jax.experimental import pallas as pl
from jax.experimental.pallas import tpu as pltpu
from jax.sharding import PartitionSpec as P

BETA = 0.8
EPS_SQUARE = 1e-30
N_DP = 4
HALF = 128
PIECE = 2 * HALF
WIDE = 512
LANES = 128
TILES = WIDE // LANES
ROWS = 128
CHUNKS = HALF // ROWS

VMEM_LIMIT = 60 * 1024 * 1024

MESH = pl.DeviceIdType.MESH
FORWARD, BACKWARD = 0, 1


def kernel(
    n_row,
    n_col,
    grad_wi,
    grad_wo,
    row_wi_hbm,
    col_wi_hbm,
    row_wo_hbm,
    col_wo_hbm,
    total,
    row_scale,
    col_scale_wi,
    col_scale_wo,
    row_wi_new,
    col_wi_new,
    row_wo_new,
    col_wo_new,
    row_wi,
    col_wi,
    row_wo,
    col_wo,
    own,
    near,
    passing,
    direct,
    combined,
    squares,
    row_part,
    col_part,
    y_one,
    z_one,
    z_two,
    x_one,
    y_two,
    x_two,
    x_three,
    y_energy,
    z_energy,
    ready,
    load_sem,
    big_send,
    passing_recv,
    direct_recv,
    combined_recv,
    gather_recv,
    onward_recv,
    small_send,
    small_recv,
):
    me = lax.axis_index("dp")
    my_row = lax.axis_index("row")
    my_col = lax.axis_index("col")
    right = lax.rem(me + 1, N_DP)
    left = lax.rem(me + N_DP - 1, N_DP)
    across = lax.rem(me + 2, N_DP)
    target = (right, left)

    def rows_at(c):
        return pl.ds(pl.multiple_of(c * ROWS, ROWS), ROWS)

    def grad_at(m, piece, start, size):
        if m == 0:
            return grad_wi.at[
                0, pl.ds(start, size), pl.ds(pl.multiple_of(piece * WIDE, WIDE), WIDE)
            ]
        return grad_wo.at[
            0, pl.ds(pl.multiple_of(piece * PIECE + start, ROWS), size), :
        ]

    def grad_chunk(m, piece, half, c):
        return grad_at(m, piece, pl.multiple_of(half * HALF + c * ROWS, ROWS), ROWS)

    loads = []
    for m in range(2):
        loads.append(pltpu.make_async_copy(grad_at(m, right, 0, HALF), near.at[FORWARD, m], load_sem.at[m]))
        loads.append(pltpu.make_async_copy(grad_at(m, left, HALF, HALF), near.at[BACKWARD, m], load_sem.at[2 + m]))
        loads.append(pltpu.make_async_copy(grad_at(m, me, 0, PIECE), own.at[m], load_sem.at[4 + m]))
    vectors = ((row_wi_hbm, row_wi), (col_wi_hbm, col_wi), (row_wo_hbm, row_wo), (col_wo_hbm, col_wo))
    for at, (source, target_ref) in enumerate(vectors):
        loads.append(pltpu.make_async_copy(source, target_ref, load_sem.at[6 + at]))
    for load in loads:
        load.start()

    barrier = pltpu.get_barrier_semaphore()

    n_y = n_row // 2
    core = lax.rem(my_row, 2)

    def beside(n):
        return [] if n == 1 else [1] if n == 2 else [1, n - 1]

    def signal(sem, axis, n, index, d):
        pl.semaphore_signal(
            sem, inc=1, device_id={axis: lax.rem(index + d, n)}, device_id_type=MESH
        )

    near_row = [2 * d for d in beside(n_y)]
    near_col = beside(n_col)
    for d in range(1, N_DP):
        signal(barrier, "dp", N_DP, me, d)
    for d in near_row:
        signal(barrier, "row", n_row, my_row, d)
    for d in near_col:
        signal(barrier, "col", n_col, my_col, d)
    pl.semaphore_signal(barrier, inc=1, device_id={"row": my_row + 1 - 2 * core}, device_id_type=MESH)
    pl.semaphore_wait(barrier, N_DP + len(near_row) + len(near_col))

    def tell(at):
        for d in near_row:
            signal(ready.at[0, at], "row", n_row, my_row, d)
        for d in near_col:
            signal(ready.at[1, at], "col", n_col, my_col, d)

    def hear(at):
        for axis, count in ((0, len(near_row)), (1, len(near_col))):
            if count:
                pl.semaphore_wait(ready.at[axis, at], count)

    def send(src, dst, send_sem, recv_sem, to):
        return pltpu.make_async_remote_copy(
            src_ref=src,
            dst_ref=dst,
            send_sem=send_sem,
            recv_sem=recv_sem,
            device_id={"dp": to},
            device_id_type=MESH,
        )

    def send_across(m):
        @pl.loop(0, CHUNKS)
        def _(c):
            for way in (FORWARD, BACKWARD):
                send(
                    grad_chunk(m, across, way, c),
                    passing.at[way, m, rows_at(c)],
                    big_send.at[0, m],
                    passing_recv.at[way, m, c],
                    target[way],
                ).start()

    def send_direct(m):
        @pl.loop(0, CHUNKS)
        def _(c):
            for way in (FORWARD, BACKWARD):
                send(
                    grad_chunk(m, target[way], 1 - way, c),
                    direct.at[way, m, rows_at(c)],
                    big_send.at[1, m],
                    direct_recv.at[way, m, c],
                    target[way],
                ).start()

    def send_combined(m):
        @pl.loop(0, CHUNKS)
        def _(c):
            for way in (FORWARD, BACKWARD):
                here = passing.at[way, m, rows_at(c)]
                send(here, here, big_send.at[0, m], passing_recv.at[way, m, c], target[way]).wait_recv()
                here[...] = (
                    here[...].astype(jnp.float32) + near[way, m, rows_at(c)].astype(jnp.float32)
                ).astype(jnp.bfloat16)
                send(
                    here,
                    combined.at[way, m, rows_at(c)],
                    big_send.at[2, m],
                    combined_recv.at[way, m, c],
                    target[way],
                ).start()

    send_across(0)
    send_direct(0)
    send_across(1)
    for load in loads:
        load.wait()
    send_combined(0)
    send_direct(1)
    send_combined(1)

    def gather(m, half, c, way):
        part = total.at[me, m, pl.ds(pl.multiple_of(half * HALF + c * ROWS, ROWS), ROWS)]
        return send(part, part, big_send.at[3 + half, m], gather_recv.at[way, m, half, c], target[way])

    def gather_start(m):
        for second in (0, 1):

            @pl.loop(0, CHUNKS)
            def _(c):
                for way in (FORWARD, BACKWARD):
                    half = 1 - way if second else way
                    gather(m, half, c, way).start()

    def own_totals(m):
        col_part[m] = jnp.zeros((8, WIDE), jnp.float32)

        @pl.loop(0, CHUNKS)
        def _(c):
            for way in (FORWARD, BACKWARD):
                first = direct.at[1 - way, m, rows_at(c)]
                second = combined.at[way, m, rows_at(c)]
                send(first, first, big_send.at[1, m], direct_recv.at[1 - way, m, c], right).wait_recv()
                send(second, second, big_send.at[2, m], combined_recv.at[way, m, c], right).wait_recv()
                rows = pl.ds(pl.multiple_of(way * HALF + c * ROWS, ROWS), ROWS)
                value = (
                    own[m, rows].astype(jnp.float32)
                    + first[...].astype(jnp.float32)
                    + second[...].astype(jnp.float32)
                )
                total[me, m, rows] = value.astype(jnp.bfloat16)
                square = value * value
                squares[m, rows] = square
                row_part[m, rows] = sum(
                    square[:, k * LANES : (k + 1) * LANES] for k in range(TILES)
                )
                col_part[m] += jnp.sum(square.reshape(ROWS // 8, 8, WIDE), axis=0)

    def exchange_start(buffer, n, axis, index, at):
        def body(j, carry):
            step = (j + 1) // 2
            d = n // 2 + step - 2 * step * lax.rem(j, 2)
            pltpu.make_async_remote_copy(
                src_ref=buffer.at[index],
                dst_ref=buffer.at[index],
                send_sem=small_send.at[at],
                recv_sem=small_recv.at[at],
                device_id={axis: lax.rem(index + d, n)},
                device_id_type=MESH,
            ).start()
            return carry

        lax.fori_loop(0, n - 1, body, 0)

    def exchange_wait(buffer, n, axis, index, at):
        others = buffer.at[pl.ds(0, n - 1)]
        pltpu.make_async_copy(others, others, small_recv.at[at]).wait()
        pltpu.make_async_copy(others, others, small_send.at[at]).wait()

    def over_col(buffer, at):
        return buffer, n_col, "col", my_col, at

    def over_row(buffer, at):
        return buffer, n_row, "row", my_row, at

    def over_dp(buffer, at):
        return buffer, N_DP, "dp", me, at

    def add_up(buffer, n):
        result = buffer[0]
        for j in range(1, n):
            result = result + buffer[j]
        return result

    def mix(previous, sums, count):
        return BETA * previous + (1.0 - BETA) * (sums * (1.0 / count) + EPS_SQUARE)

    def down(x):
        return jnp.broadcast_to(x, (LANES, LANES)).T

    def fold_rows(part):
        halves = [part[half * HALF : (half + 1) * HALF].T for half in range(2)]
        return jnp.concatenate([jnp.sum(x, axis=0, keepdims=True) for x in halves], axis=0)

    def row_sums(m):
        return fold_rows(row_part[m])

    def col_sums(m):
        column = jnp.sum(col_part[m], axis=0, keepdims=True)
        return jnp.concatenate([column[:, k * LANES : (k + 1) * LANES] for k in range(TILES)], axis=0)

    def weighted_row_sums(m, inverse):
        return fold_rows(
            sum(squares[m, :, k * LANES : (k + 1) * LANES] * inverse[k : k + 1] for k in range(TILES))
        )

    def weighted_col_sums(m, inverse):
        weights = [down(inverse[half : half + 1]) for half in range(2)]
        result = []
        for k in range(TILES):
            part = jnp.zeros((8, LANES), jnp.float32)
            for half in range(2):
                x = squares[m, half * HALF : (half + 1) * HALF, k * LANES : (k + 1) * LANES] * weights[half]
                part += jnp.sum(x.reshape(HALF // 8, 8, LANES), axis=0)
            result.append(jnp.sum(part, axis=0, keepdims=True))
        return jnp.concatenate(result, axis=0)

    def onward(m):
        @pl.loop(0, CHUNKS)
        def _(c):
            for way in (FORWARD, BACKWARD):
                source = target[1 - way]
                half = way
                part = total.at[source, m, pl.ds(pl.multiple_of(half * HALF + c * ROWS, ROWS), ROWS)]
                send(part, part, big_send.at[3, m], gather_recv.at[way, m, half, c], right).wait_recv()
                send(part, part, big_send.at[5, m], onward_recv.at[way, m, c], target[way]).start()

    rows_wi, rows_wo = n_row * PIECE, n_row * PIECE * N_DP
    cols_wi, cols_wo = n_col * WIDE * N_DP, n_col * WIDE

    tell(0)
    hear(0)
    tell(1)
    hear(1)
    tell(2)
    hear(2)
    tell(3)
    own_totals(0)
    hear(3)
    y_one[my_row] = col_sums(0)
    exchange_start(*over_row(y_one, 0))
    pltpu.make_async_copy(passing.at[0], passing.at[0], big_send.at[2, 1]).wait()
    gather_start(0)
    own_totals(1)
    z_one[my_col] = row_sums(1)
    exchange_start(*over_col(z_one, 1))
    gather_start(1)

    exchange_wait(*over_row(y_one, 0))
    col_sums_wi = add_up(y_one, n_row)
    own_col_wi = mix(col_wi[pl.ds(me * TILES, TILES)], col_sums_wi, rows_wi)
    z_two[my_col] = jnp.concatenate(
        [row_sums(0), weighted_row_sums(0, 1.0 / own_col_wi)], axis=0
    )
    exchange_start(*over_col(z_two, 2))
    y_two[my_row, 0:4] = col_sums(1)
    exchange_wait(*over_col(z_one, 1))
    row_sums_wo = add_up(z_one, n_col)
    own_row_wo = mix(row_wo[pl.ds(me * 2, 2)], row_sums_wo, cols_wo)
    y_two[my_row, 4:8] = weighted_col_sums(1, 1.0 / own_row_wo)
    exchange_start(*over_row(y_two, 4))

    exchange_wait(*over_col(z_two, 2))
    x_one[me] = jnp.concatenate([add_up(z_two, n_col), col_sums_wi], axis=0)
    exchange_start(*over_dp(x_one, 3))
    exchange_wait(*over_row(y_two, 4))
    x_two[me] = add_up(y_two, n_row)
    exchange_start(*over_dp(x_two, 5))
    x_three[me] = row_sums_wo
    exchange_start(*over_dp(x_three, 8))
    onward(0)
    onward(1)
    exchange_wait(*over_dp(x_one, 3))
    sums = x_one[0, 0:4] + x_one[1, 0:4] + x_one[2, 0:4] + x_one[3, 0:4]
    new_row_wi = mix(row_wi[...], sums[0:2], cols_wi)
    energy = jnp.sum(sums[2:4] / new_row_wi, axis=0, keepdims=True)
    y_energy[my_row] = jnp.concatenate([energy, energy], axis=0)
    exchange_start(*over_row(y_energy, 6))
    exchange_wait(*over_dp(x_two, 5))
    sums = add_up(x_two, N_DP)
    new_col_wo = mix(col_wo[...], sums[0:4], rows_wo)
    energy = jnp.sum(sums[4:8] / new_col_wo, axis=0, keepdims=True)
    z_energy[my_col] = jnp.concatenate([energy, energy], axis=0)
    exchange_start(*over_col(z_energy, 7))

    row_wi_new[...] = new_row_wi
    factor = lax.rsqrt(new_row_wi)
    for half in range(2):
        row_scale[half] = down(factor[half : half + 1])
    exchange_wait(*over_dp(x_three, 8))
    new = mix(row_wo[...], jnp.concatenate([x_three[x] for x in range(N_DP)], axis=0), cols_wo)
    row_wo_new[...] = new
    factor = lax.rsqrt(new)
    for half in range(2 * N_DP):
        row_scale[2 + half] = down(factor[half : half + 1])
    new = mix(col_wi[...], jnp.concatenate([x_one[x, 4:8] for x in range(N_DP)], axis=0), rows_wi)
    col_wi_new[...] = new
    factor_wi = lax.rsqrt(new)
    col_wo_new[...] = new_col_wo
    factor_wo = lax.rsqrt(new_col_wo)

    def clip(sums):
        energy = jnp.sum(sums[0:1], axis=1, keepdims=True)
        return 1.0 / jnp.maximum(1.0, jnp.sqrt(energy * (1.0 / (rows_wi * cols_wi))))

    exchange_wait(*over_row(y_energy, 6))
    col_scale_wi[...] = factor_wi * clip(add_up(y_energy, n_row))
    exchange_wait(*over_col(z_energy, 7))
    col_scale_wo[...] = factor_wo * clip(add_up(z_energy, n_col))

    for m in range(2):

        @pl.loop(0, CHUNKS)
        def _(c):
            for way in (FORWARD, BACKWARD):
                half = 1 - way
                part = total.at[target[1 - way], m, pl.ds(pl.multiple_of(half * HALF + c * ROWS, ROWS), ROWS)]
                send(part, part, big_send.at[3, m], gather_recv.at[way, m, half, c], right).wait_recv()
                part = total.at[across, m, pl.ds(pl.multiple_of(way * HALF + c * ROWS, ROWS), ROWS)]
                send(part, part, big_send.at[5, m], onward_recv.at[way, m, c], right).wait_recv()

    for at in range(6):
        for m in range(2):
            if (at, m) != (2, 1):
                pltpu.make_async_copy(passing.at[0], passing.at[0], big_send.at[at, m]).wait()


def finish(
    total,
    row_scale,
    col_scale_wi,
    col_scale_wo,
    row_wi_new,
    col_wi_new,
    row_wo_new,
    col_wo_new,
    update_wi,
    row_wi_out,
    col_wi_out,
    update_wo,
    row_wo_out,
    col_wo_out,
    ready_wi,
    ready_wo,
    small_sem,
    big_sem,
):
    small = [
        pltpu.make_async_copy(source, result, small_sem.at[at])
        for at, (source, result) in enumerate(
            (
                (row_wi_new, row_wi_out),
                (col_wi_new, col_wi_out),
                (row_wo_new, row_wo_out),
                (col_wo_new, col_wo_out),
            )
        )
    ]
    for copy in small:
        copy.start()

    def block(m, piece, half):
        if m == 0:
            at = (
                pl.ds(pl.multiple_of(half * HALF, HALF), HALF),
                pl.ds(pl.multiple_of(piece * WIDE, WIDE), WIDE),
            )
            return ready_wi.at[at], update_wi.at[at]
        at = pl.ds(pl.multiple_of(piece * PIECE + half * HALF, HALF), HALF)
        return ready_wo.at[at], update_wo.at[at]

    def write(m, piece, half):
        source, result = block(m, piece, half)
        return pltpu.make_async_copy(source, result, big_sem.at[m, piece, half])

    for m in range(2):

        @pl.loop(0, 2 * N_DP)
        def _(step):
            piece, half = step // 2, step % 2
            ready = block(m, piece, half)[0]
            rows = pl.ds(pl.multiple_of(half * HALF, HALF), HALF)
            value = total[piece, m, rows].astype(jnp.float32)
            scale = row_scale[half] if m == 0 else row_scale[2 + step]
            for k in range(TILES):
                if m == 0:
                    column = col_scale_wi[pl.ds(piece * TILES + k, 1)]
                else:
                    column = col_scale_wo[k : k + 1]
                part = slice(k * LANES, (k + 1) * LANES)
                ready[:, part] = (value[:, part] * scale * column).astype(jnp.bfloat16)
            write(m, piece, half).start()

    for copy in small:
        copy.wait()
    for m in range(2):

        @pl.loop(0, 2 * N_DP)
        def _(step):
            write(m, step // 2, step % 2).wait()


def local(n_row, n_col, grad_wi, grad_wo, row_wi, col_wi, row_wo, col_wo):
    vmem = pl.BlockSpec(memory_space=pltpu.VMEM)
    hbm = pl.BlockSpec(memory_space=pltpu.HBM)
    f32, bf16 = jnp.float32, jnp.bfloat16

    def folded(x):
        return x.reshape(x.shape[0] // LANES, LANES)

    vectors = [folded(x) for x in (row_wi, col_wi, row_wo, col_wo)]
    out = pl.pallas_call(
        functools.partial(kernel, n_row, n_col),
        out_shape=(
            pltpu.VMEM((N_DP, 2, PIECE, WIDE), bf16),
            pltpu.VMEM((2 + 2 * N_DP, LANES, LANES), f32),
            pltpu.VMEM(vectors[1].shape, f32),
            pltpu.VMEM(vectors[3].shape, f32),
        )
        + tuple(pltpu.VMEM(x.shape, f32) for x in vectors),
        in_specs=[hbm] * 6,
        out_specs=[vmem] * 8,
        scratch_shapes=[pltpu.VMEM(x.shape, f32) for x in vectors]
        + [
            pltpu.VMEM((2, PIECE, WIDE), bf16),
            pltpu.VMEM((2, 2, HALF, WIDE), bf16),
            pltpu.VMEM((2, 2, HALF, WIDE), bf16),
            pltpu.VMEM((2, 2, HALF, WIDE), bf16),
            pltpu.VMEM((2, 2, HALF, WIDE), bf16),
            pltpu.VMEM((2, PIECE, WIDE), f32),
            pltpu.VMEM((2, PIECE, LANES), f32),
            pltpu.VMEM((2, 8, WIDE), f32),
            pltpu.VMEM((n_row, 4, LANES), f32),
            pltpu.VMEM((n_col, 2, LANES), f32),
            pltpu.VMEM((n_col, 4, LANES), f32),
            pltpu.VMEM((N_DP, 8, LANES), f32),
            pltpu.VMEM((n_row, 8, LANES), f32),
            pltpu.VMEM((N_DP, 8, LANES), f32),
            pltpu.VMEM((N_DP, 2, LANES), f32),
            pltpu.VMEM((n_row, 2, LANES), f32),
            pltpu.VMEM((n_col, 2, LANES), f32),
            pltpu.SemaphoreType.REGULAR((2, 4)),
            pltpu.SemaphoreType.DMA((10,)),
            pltpu.SemaphoreType.DMA((6, 2)),
            pltpu.SemaphoreType.DMA((2, 2, CHUNKS)),
            pltpu.SemaphoreType.DMA((2, 2, CHUNKS)),
            pltpu.SemaphoreType.DMA((2, 2, CHUNKS)),
            pltpu.SemaphoreType.DMA((2, 2, 2, CHUNKS)),
            pltpu.SemaphoreType.DMA((2, 2, CHUNKS)),
            pltpu.SemaphoreType.DMA((9,)),
            pltpu.SemaphoreType.DMA((9,)),
        ],
        compiler_params=pltpu.CompilerParams(
            collective_id=0, has_side_effects=True, vmem_limit_bytes=VMEM_LIMIT
        ),
        name="adafactor",
    )(grad_wi, grad_wo, *vectors)
    out = pl.pallas_call(
        finish,
        out_shape=(
            jax.ShapeDtypeStruct(grad_wi.shape[1:], bf16),
            jax.ShapeDtypeStruct(vectors[0].shape, f32),
            jax.ShapeDtypeStruct(vectors[1].shape, f32),
            jax.ShapeDtypeStruct(grad_wo.shape[1:], bf16),
            jax.ShapeDtypeStruct(vectors[2].shape, f32),
            jax.ShapeDtypeStruct(vectors[3].shape, f32),
        ),
        in_specs=[vmem] * 8,
        out_specs=[hbm] * 6,
        scratch_shapes=[
            pltpu.VMEM(grad_wi.shape[1:], bf16),
            pltpu.VMEM(grad_wo.shape[1:], bf16),
            pltpu.SemaphoreType.DMA((4,)),
            pltpu.SemaphoreType.DMA((2, N_DP, 2)),
        ],
        compiler_params=pltpu.CompilerParams(vmem_limit_bytes=6 * 1024 * 1024),
        name="finish",
    )(*[pltpu.with_memory_space_constraint(x, pltpu.VMEM) for x in out])
    return (
        out[0],
        out[1].reshape(row_wi.shape),
        out[2].reshape(col_wi.shape),
        out[3],
        out[4].reshape(row_wo.shape),
        out[5].reshape(col_wo.shape),
    )


def solution(mesh):
    return jax.shard_map(
        functools.partial(local, mesh.shape["row"], mesh.shape["col"]),
        mesh=mesh,
        in_specs=(
            P("dp", "row", "col"),
            P("dp", "row", "col"),
            P("row"),
            P("col"),
            P("row"),
            P("col"),
        ),
        out_specs=(P("row", "col"), P("row"), P("col"), P("row", "col"), P("row"), P("col")),
        check_vma=False,
    )
```
